32 devices in a mesh: ops: 8 (over y, x, core), sec: 4 (over z).
Axes of the slice: x: 2, y: 2, z: 4, core: 2. Of those that a mesh axis runs over, the one named last changes fastest.
Arguments:
- psi: float32 [4, 512, 512], P('sec')
- left_ops: float32 [32, 4, 512, 512], P('ops', 'sec')
- right_ops: float32 [32, 4, 512, 512], P('ops', 'sec')
- links: int32 [32, 4], P('ops', 'sec'), may hold values from 0 to 4, as said below
Outputs:
- sigma: float32 [4, 512, 512], P('sec', 'ops')
- direction: float32 [4, 512, 512], P('sec', 'ops')
- energies: float32 [2], replicated
The draws below stay inside these ranges and needn't reach their ends.
Inputs may be any that keep to these rules, and one draw needn't show every extreme that they name: `links`: A value of 4 means that the term has no block on that source sector.
All inputs are finite; a program needn't handle non-finite values.
Results may differ from the reference program's by a relative error of at most 0.0003.
Values sent between devices are 32-bit elements; how exact they have to be, the bound alone decides.
No kernel may reach another device: no remote copies, remote signals or barrier semaphores. Data moves between devices by JAX's collectives and lax.ppermute only.
A program may use at most 64 MiB of HBM per device.

```python
import jax
import jax.numpy as jnp
from jax import lax

M = 512
TERMS = 32
S = 4


def operator_blocks(key, diag_low, diag_high, off_scale):
    diag_key, offdiagonal_key = jax.random.split(key)
    diagonal_part = jnp.exp(jax.random.uniform(diag_key, (TERMS, S, M), jnp.float32, jnp.log(diag_low), jnp.log(diag_high)))
    off_part = jnp.clip(jax.random.normal(offdiagonal_key, (TERMS, S, M, M), jnp.float32), -4.0, 4.0) * (off_scale / M ** 0.5)
    identity = jnp.eye(M, dtype=jnp.float32)
    blocks = identity * diagonal_part[..., None] + off_part
    return blocks * TERMS ** (-0.25)


def draw_left_ops(key, part):
    key = jax.random.fold_in(key, 1)
    return operator_blocks(key, 0.5, 2.0, 1.0)


def draw_right_ops(key, part):
    key = jax.random.fold_in(key, 2)
    return operator_blocks(key, 0.5, 2.0, 1.0)


def draw_psi(key, part):
    key = jax.random.fold_in(key, 3)
    value_key, row_key = jax.random.split(key)
    sector_scale = 1.0 + 2.0 * jnp.arange(S).astype(jnp.float32) / (S - 1)
    values = jnp.clip(jax.random.normal(value_key, (S, M, M), jnp.float32), -4.0, 4.0)
    row_scale = jnp.exp(jax.random.uniform(row_key, (S, M, 1), jnp.float32, 0.0, jnp.log(4.0)))
    return values * row_scale * sector_scale[:, None, None]


def draw_links(key, part):
    key = jax.random.fold_in(key, 7)
    mode_key, limit_key, same_key, other_key = jax.random.split(key, 4)
    mode = jax.random.randint(mode_key, (TERMS, S), 0, 4)
    limit = jax.random.randint(limit_key, (TERMS, 1), 1, 5)
    same = jax.random.randint(same_key, (TERMS, S), 0, 2)
    other = jax.random.randint(other_key, (TERMS, S), 0, S)
    source = jnp.arange(S, dtype=jnp.int32)[None, :]
    target = jnp.where(same == 0, source, other)
    return jnp.where(mode < limit, target, S).astype(jnp.int32)


def setup_inputs(seed: int = 0) -> dict:
    keys = jax.random.split(jax.random.key(seed), 5)
    psi = draw_psi(jax.random.fold_in(keys[4], 71), 0)
    left_ops = draw_left_ops(jax.random.fold_in(keys[4], 71), 0)
    right_ops = draw_right_ops(jax.random.fold_in(keys[4], 71), 0)
    links = draw_links(jax.random.fold_in(keys[4], 71), 0)
    return {"psi": psi, "left_ops": left_ops, "right_ops": right_ops, "links": links}


def reference(psi, left_ops, right_ops, links):
    highest = lax.Precision.HIGHEST
    sector_ids = jnp.arange(S).astype(jnp.int32)

    def one_term(total, term_data):
        lefts, right_blocks, targets = term_data

        def one_sector(inner, sector_data):
            left, right, target, source = sector_data
            product_left = jnp.dot(left, source, precision=highest, preferred_element_type=jnp.float32)
            product_full = jnp.dot(product_left, right.T, precision=highest, preferred_element_type=jnp.float32)
            selector = (sector_ids == target).astype(jnp.float32)
            return (inner + selector[:, None, None] * product_full[None], None)
        total, _ = lax.scan(one_sector, total, (lefts, right_blocks, targets, psi))
        return (total, None)
    sigma, _ = lax.scan(one_term, jnp.zeros((S, M, M), jnp.float32), (left_ops, right_ops, links))
    correlation = jnp.sum(psi * sigma)
    weight = jnp.sum(psi * psi)
    theta = correlation / weight
    residual_vector = sigma - theta * psi
    residual_squared = jnp.sum(residual_vector * residual_vector)
    norm_scale_factor = jnp.sqrt(residual_squared)
    direction = residual_vector / norm_scale_factor
    energies = jnp.stack([theta, norm_scale_factor])
    return (sigma, direction, energies)
```

```python
import functools

import jax
import jax.numpy as jnp
from jax import lax
from jax.experimental import pallas as pl
from jax.experimental.pallas import tpu as pltpu
from jax.sharding import PartitionSpec as P

PIECES = (32, 32)

NT = (((1,), (1,)), ((), ()))
NN = (((1,), (0,)), ((), ()))


def log2(n):
    bits = n.bit_length() - 1
    assert n == 1 << bits
    return bits


def bit_orders(bits):
    first = list(range(1, bits))
    turn = (bits - 1) // 2
    return first, first[turn:] + first[:turn]


def split(x):
    high = x.astype(jnp.bfloat16)
    low = (x - high.astype(jnp.float32)).astype(jnp.bfloat16)
    return high, low


def dot3(a, b_high, b_low, dims):
    a_high, a_low = split(a)
    rows = a.shape[0]
    both = lax.dot_general(
        jnp.concatenate([a_high, a_low], 0), b_high, dims, preferred_element_type=jnp.float32
    )
    cross = lax.dot_general(a_high, b_low, dims, preferred_element_type=jnp.float32)
    return both[:rows] + (both[rows:] + cross)


def sigma_kernel(orders, ops_bits, sectors, links_ref, psi_ref, left_ref, right_ref, keep_ref, send_ref, psi_high, psi_low):
    pair = pl.program_id(0)
    rows, states = left_ref.shape[2:]
    slots = 1 << (ops_bits - 1)
    me = lax.axis_index("ops")
    core = me & 1

    @pl.when(pair == 0)
    def _():
        keep_ref[...] = jnp.zeros_like(keep_ref)
        send_ref[...] = jnp.zeros_like(send_ref)
        high, low = split(psi_ref[0])
        psi_high[...] = high
        psi_low[...] = low

    target = links_ref[pair, 0]

    @pl.when(target < sectors)
    def _():
        slot = target ^ lax.axis_index("sec")
        blocks = []
        for away in range(2):
            owner_core = core ^ away
            for q in range(slots):
                masks = [
                    sum(1 << order[step] for step in range(ops_bits - 1) if (q >> (ops_bits - 2 - step)) & 1)
                    for order in orders
                ]
                block = me ^ away ^ jnp.where(owner_core == 0, masks[0], masks[1])
                blocks.append(left_ref[0, block])
        product_left = dot3(jnp.concatenate(blocks, 0), psi_high[...], psi_low[...], NN)
        right_high, right_low = split(right_ref[0])
        product = dot3(product_left, right_high, right_low, NT)
        product = product.reshape(2, slots, rows, states)
        for q in range(slots):
            keep_ref[q, slot] += product[0, q]
            send_ref[q, slot] += product[1, q]


def partial_sigma(psi, lefts, rights, links, piece, start, ops_bits, sectors):
    pairs, owners, rows, states = lefts.shape
    slots = owners // 2
    out = jax.ShapeDtypeStruct((slots, sectors, piece, states), jnp.float32)
    whole = pl.BlockSpec((slots, sectors, piece, states), lambda p: (0, 0, 0, 0))
    return pl.pallas_call(
        functools.partial(sigma_kernel, bit_orders(ops_bits), ops_bits, sectors),
        grid=(pairs,),
        in_specs=[
            pl.BlockSpec(memory_space=pltpu.SMEM),
            pl.BlockSpec((1, states, states), lambda p: (0, 0, 0)),
            pl.BlockSpec((1, owners, piece, states), lambda p: (p, 0, start // piece, 0)),
            pl.BlockSpec((1, states, states), lambda p: (p, 0, 0)),
        ],
        out_specs=[whole, whole],
        out_shape=[out, out],
        scratch_shapes=[pltpu.VMEM((states, states), jnp.bfloat16)] * 2,
        compiler_params=pltpu.CompilerParams(
            dimension_semantics=("arbitrary",), vmem_limit_bytes=48 * 2**20
        ),
        cost_estimate=pl.CostEstimate(
            flops=12 * pairs * owners * piece * states * states,
            bytes_accessed=4 * (pairs * states * states + owners * piece * states * (pairs + sectors)),
            transcendentals=0,
        ),
        name="partial_sigma",
    )(links, psi, lefts, rights)


def stats_kernel(psi_ref, sigma_ref, stats_ref):
    psi = psi_ref[0]
    sigma = sigma_ref[0]
    weight = jnp.sum(psi * psi)
    correlation = jnp.sum(psi * sigma)
    theta = jnp.where(weight > 0.0, correlation / weight, 0.0)
    residual = sigma - theta * psi
    squared = jnp.sum(residual * residual)
    lane = lax.broadcasted_iota(jnp.int32, stats_ref.shape, 1)
    stats_ref[...] = jnp.where(lane == 0, weight, jnp.where(lane == 1, theta, jnp.where(lane == 2, squared, 0.0)))


def finish_kernel(psi_ref, sigma_ref, stats_ref, direction_ref, energies_ref):
    weights = stats_ref[:, 0:1]
    thetas = stats_ref[:, 1:2]
    squares = stats_ref[:, 2:3]
    theta = jnp.sum(weights * thetas) / jnp.sum(weights)
    apart = thetas - theta
    norm = jnp.sqrt(jnp.sum(squares + weights * apart * apart))
    direction_ref[0] = (sigma_ref[0] - theta * psi_ref[0]) / norm
    lane = lax.broadcasted_iota(jnp.int32, energies_ref.shape, 1)
    energies_ref[...] = jnp.where(lane == 0, theta, norm)


def local(psi, left_ops, right_ops, links):
    ops_width = lax.axis_size("ops")
    sectors = lax.axis_size("sec")
    ops_bits = log2(ops_width)
    log2(sectors)
    pairs, _, states, _ = left_ops.shape
    rows = states // ops_width
    lefts = left_ops.reshape(pairs, ops_width, rows, states)
    rights = right_ops.reshape(pairs, states, states)
    orders = bit_orders(ops_bits)
    pieces = PIECES if sum(PIECES) == rows else (rows // 2, rows // 2)
    sigma_pieces = []
    start = 0
    for piece in pieces:
        keep, send = partial_sigma(psi, lefts, rights, links, piece, start, ops_bits, sectors)
        start += piece
        parts = [keep, lax.ppermute(send, "ops", [(i, i ^ 1) for i in range(ops_width)])]
        for step in range(ops_bits - 1):
            half = parts[0].shape[0] // 2
            partner = [(i, i ^ (1 << orders[i & 1][step])) for i in range(ops_width)]
            came = lax.ppermute(sum(p[half:] for p in parts), "ops", partner)
            parts = [p[:half] for p in parts] + [came]
        parts = [p[0] for p in parts]
        mine = sum(p[0] for p in parts)
        for q in range(1, sectors):
            mine = mine + lax.ppermute(sum(p[q] for p in parts), "sec", [(i, i ^ q) for i in range(sectors)])
        sigma_pieces.append(mine)
    sigma = jnp.concatenate(sigma_pieces, 0)[None]
    index = lax.axis_index("ops")
    psi_rows = lax.dynamic_slice_in_dim(psi, index * rows, rows, 1)
    devices = ops_width * sectors
    stats = pl.pallas_call(
        stats_kernel,
        out_shape=jax.ShapeDtypeStruct((devices, 128), jnp.float32),
        name="stats",
    )(psi_rows, sigma)
    stats = lax.all_to_all(stats, ("ops", "sec"), 0, 0, tiled=True)
    direction, energies = pl.pallas_call(
        finish_kernel,
        out_shape=[
            jax.ShapeDtypeStruct((1, rows, states), jnp.float32),
            jax.ShapeDtypeStruct((1, 128), jnp.float32),
        ],
        name="finish",
    )(psi_rows, sigma, stats)
    return (sigma, direction, energies[0, :2])


def solution(mesh):
    return jax.shard_map(
        local,
        mesh=mesh,
        in_specs=(
            P("sec", None, None),
            P("ops", "sec", None, None),
            P("ops", "sec", None, None),
            P("ops", "sec"),
        ),
        out_specs=(P("sec", "ops", None), P("sec", "ops", None), P()),
        check_vma=False,
    )
```

```python
import functools

import jax
import jax.numpy as jnp
from jax import lax
from jax.experimental import pallas as pl
from jax.experimental.pallas import tpu as pltpu
from jax.sharding import PartitionSpec as P

PIECES = (32, 32)

VMEM_BYTES = 32 * 2**20
FIFO = False
DIRECT = (True,)

NT = (((1,), (1,)), ((), ()))
NN = (((1,), (0,)), ((), ()))


def log2(n):
    bits = n.bit_length() - 1
    assert n == 1 << bits
    return bits


def bit_orders(bits):
    first = list(range(1, bits))
    turn = (bits - 1) // 2
    return first, first[turn:] + first[:turn]


def split(x):
    high = x.astype(jnp.bfloat16)
    low = (x - high.astype(jnp.float32)).astype(jnp.bfloat16)
    return high, low


def dot3(a, b_high, b_low, dims):
    a_high, a_low = split(a)
    rows = a.shape[0]
    both = lax.dot_general(
        jnp.concatenate([a_high, a_low], 0), b_high, dims, preferred_element_type=jnp.float32
    )
    cross = lax.dot_general(a_high, b_low, dims, preferred_element_type=jnp.float32)
    return both[:rows] + (both[rows:] + cross)


def sigma_kernel(
    orders, ops_bits, sectors, pieces, links_ref, psi_ref, lefts_ref, rights_ref, *rest
):
    outs = rest[: 2 * len(pieces)]
    psi, lefts, rights, psi_high, psi_low, targets, sems = rest[2 * len(pieces) :]
    pairs, _, rows, states = lefts.shape
    slots = 1 << (ops_bits - 1)
    me = lax.axis_index("ops")
    core = me & 1
    psi_copy = pltpu.make_async_copy(psi_ref.at[0], psi, sems.at[2 * pairs])
    links_copy = pltpu.make_async_copy(links_ref, targets, sems.at[2 * pairs + 1])
    left_copies = [pltpu.make_async_copy(lefts_ref.at[p], lefts.at[p], sems.at[p]) for p in range(pairs)]
    right_copies = [pltpu.make_async_copy(rights_ref.at[p], rights.at[p], sems.at[pairs + p]) for p in range(pairs)]
    links_copy.start()
    psi_copy.start()
    for p in range(pairs):
        left_copies[p].start()
        right_copies[p].start()
    for out in outs:
        out[...] = jnp.zeros_like(out)
    links_copy.wait()
    psi_copy.wait()
    high, low = split(psi[...])
    psi_high[...] = high
    psi_low[...] = low

    def contribute(pair, slot):
        blocks = []
        for away in range(2):
            owner_core = core ^ away
            for q in range(slots):
                masks = [
                    sum(1 << order[step] for step in range(ops_bits - 1) if (q >> (ops_bits - 2 - step)) & 1)
                    for order in orders
                ]
                block = me ^ away ^ jnp.where(owner_core == 0, masks[0], masks[1])
                blocks.append(lefts[pair, block])
        product_left = dot3(jnp.concatenate(blocks, 0), psi_high[...], psi_low[...], NN)
        right_high, right_low = split(rights[pair])
        product = dot3(product_left, right_high, right_low, NT)
        product = product.reshape(2, slots, rows, states)
        start = 0
        for piece, keep_ref, send_ref in zip(pieces, outs[::2], outs[1::2]):
            for q in range(slots):
                keep_ref[q, slot] += product[0, q, start : start + piece]
                send_ref[q, slot] += product[1, q, start : start + piece]
            start += piece

    for p in range(pairs):
        left_copies[p].wait()
        right_copies[p].wait()
        target = targets[p]

        @pl.when(target < sectors)
        def _():
            contribute(p, target ^ lax.axis_index("sec"))


def partial_sigma(psi, lefts, rights, links, pieces, ops_bits, sectors):
    pairs, owners, rows, states = lefts.shape
    outs = [jax.ShapeDtypeStruct((owners // 2, sectors, piece, states), jnp.float32) for piece in pieces for _ in range(2)]
    return pl.pallas_call(
        functools.partial(sigma_kernel, bit_orders(ops_bits), ops_bits, sectors, pieces),
        in_specs=[pl.BlockSpec(memory_space=pltpu.HBM)] * 4,
        out_specs=[pl.BlockSpec(memory_space=pltpu.VMEM)] * len(outs),
        out_shape=outs,
        scratch_shapes=[
            pltpu.VMEM((states, states), jnp.float32),
            pltpu.VMEM((pairs, owners, rows, states), jnp.float32),
            pltpu.VMEM((pairs, states, states), jnp.float32),
            pltpu.VMEM((states, states), jnp.bfloat16),
            pltpu.VMEM((states, states), jnp.bfloat16),
            pltpu.SMEM((pairs,), jnp.int32),
            pltpu.SemaphoreType.DMA((2 * pairs + 2,)),
        ],
        compiler_params=pltpu.CompilerParams(vmem_limit_bytes=VMEM_BYTES),
        cost_estimate=pl.CostEstimate(
            flops=12 * pairs * owners * rows * states * states,
            bytes_accessed=4 * states * states * (2 * pairs + 1),
            transcendentals=0,
        ),
        name="partial_sigma",
    )(*[pltpu.with_memory_space_constraint(x, pltpu.HBM) for x in (links, psi, lefts, rights)])


def stats_kernel(groups, psi_ref, *rest):
    ins, (sigma_ref, held_ref, psi_rows_ref, stats_ref, sem) = rest[:-5], rest[-5:]
    rows = sigma_ref.shape[1]
    copy = pltpu.make_async_copy(
        psi_ref.at[0, pl.ds(pl.multiple_of(lax.axis_index("ops") * rows, rows), rows)], psi_rows_ref, sem
    )
    copy.start()
    at = 0
    start = 0
    for group in groups:
        total = ins[at][...]
        for ref in ins[at + 1 : at + group]:
            total = total + ref[...]
        at += group
        total = total.reshape(total.shape[-2:])
        held_ref[start : start + total.shape[0]] = total
        start += total.shape[0]
    copy.wait()
    psi = psi_rows_ref[...]
    sigma = held_ref[...]
    sigma_ref[0] = sigma
    weight = jnp.sum(psi * psi)
    correlation = jnp.sum(psi * sigma)
    theta = jnp.where(weight > 0.0, correlation / weight, 0.0)
    residual = sigma - theta * psi
    squared = jnp.sum(residual * residual)
    lane = lax.broadcasted_iota(jnp.int32, stats_ref.shape, 1)
    stats_ref[...] = jnp.where(lane == 0, weight, jnp.where(lane == 1, theta, jnp.where(lane == 2, squared, 0.0)))


def finish_kernel(psi_ref, sigma_ref, stats_ref, direction_ref, energies_ref):
    weights = stats_ref[:, 0:1]
    thetas = stats_ref[:, 1:2]
    squares = stats_ref[:, 2:3]
    theta = jnp.sum(weights * thetas) / jnp.sum(weights)
    apart = thetas - theta
    norm = jnp.sqrt(jnp.sum(squares + weights * apart * apart))
    energies_ref[0] = theta
    energies_ref[1] = norm
    direction_ref[0] = (sigma_ref[...] - theta * psi_ref[...]) / norm


def after(value, earlier):
    if earlier is None:
        return value
    return lax.optimization_barrier((value, earlier))[0]


def local(psi, left_ops, right_ops, links):
    ops_width = lax.axis_size("ops")
    sectors = lax.axis_size("sec")
    ops_bits = log2(ops_width)
    sec_bits = log2(sectors)
    pairs, _, states, _ = left_ops.shape
    rows = states // ops_width
    lefts = left_ops.reshape(pairs, ops_width, rows, states)
    rights = right_ops.reshape(pairs, states, states)
    links = links.reshape(pairs)
    orders = bit_orders(ops_bits)
    pieces = PIECES if sum(PIECES) == rows else (rows // 2, rows // 2)
    partials = partial_sigma(psi, lefts, rights, links, pieces, ops_bits, sectors)
    terms = []
    groups = []
    came = None
    for index, keep, send in zip(range(len(pieces)), partials[::2], partials[1::2]):
        parts = [keep, lax.ppermute(send, "ops", [(i, i ^ 1) for i in range(ops_width)])]
        for step in range(ops_bits - 1):
            half = parts[0].shape[0] // 2
            partner = [(i, i ^ (1 << orders[i & 1][step])) for i in range(ops_width)]
            leaving = sum(p[half:] for p in parts)
            if step == 0 and FIFO:
                leaving = after(leaving, came)
            arrived = lax.ppermute(leaving, "ops", partner)
            if step == 0:
                came = arrived
            parts = [p[:half] for p in parts] + [arrived]
        parts = [p[0] for p in parts]
        if DIRECT[index % len(DIRECT)]:
            parts += [
                lax.ppermute(sum(p[q] for p in parts), "sec", [(i, i ^ q) for i in range(sectors)])
                for q in range(1, sectors)
            ]
        else:
            for bit in range(sec_bits):
                low = sectors >> (sec_bits - bit)
                picked = [q for q in range(sectors) if q & ((1 << (bit + 1)) - 1) == 1 << bit]
                kept = [q for q in range(sectors) if q & ((1 << (bit + 1)) - 1) == 0]
                if bit == 0:
                    parts = [[p[q] for q in range(sectors)] for p in parts]
                leaving = jnp.stack([sum(p[q] for p in parts) for q in picked])
                arrived = lax.ppermute(leaving, "sec", [(i, i ^ (1 << bit)) for i in range(sectors)])
                slot = dict(zip(kept, range(len(kept))))
                parts = parts + [[arrived[slot[q]] if q in slot else None for q in range(sectors)]]
            parts = [p[0][None] for p in parts]
        terms += [p[0] for p in parts[: len(parts)]] if not DIRECT[index % len(DIRECT)] else [p[0] if p.ndim == 3 else p for p in parts]
        groups.append(len(parts))
    devices = ops_width * sectors
    vmem = pl.BlockSpec(memory_space=pltpu.VMEM)
    sigma, held, psi_rows, stats = pl.pallas_call(
        functools.partial(stats_kernel, groups),
        in_specs=[pl.BlockSpec(memory_space=pltpu.HBM)] + [vmem] * len(terms),
        out_specs=[vmem] * 4,
        out_shape=[
            jax.ShapeDtypeStruct((1, rows, states), jnp.float32),
            jax.ShapeDtypeStruct((rows, states), jnp.float32),
            jax.ShapeDtypeStruct((rows, states), jnp.float32),
            jax.ShapeDtypeStruct((devices, 128), jnp.float32),
        ],
        scratch_shapes=[pltpu.SemaphoreType.DMA],
        compiler_params=pltpu.CompilerParams(vmem_limit_bytes=8 * 2**20),
        name="stats",
    )(psi, *terms)
    stats = lax.all_to_all(stats, ("ops", "sec"), 0, 0, tiled=True)
    direction, energies = pl.pallas_call(
        finish_kernel,
        in_specs=[vmem] * 3,
        out_specs=[vmem, pl.BlockSpec(memory_space=pltpu.SMEM)],
        out_shape=[
            jax.ShapeDtypeStruct((1, rows, states), jnp.float32),
            jax.ShapeDtypeStruct((2,), jnp.float32),
        ],
        compiler_params=pltpu.CompilerParams(vmem_limit_bytes=4 * 2**20),
        name="finish",
    )(psi_rows, held, stats)
    return (sigma, direction, energies)


def solution(mesh):
    return jax.shard_map(
        local,
        mesh=mesh,
        in_specs=(
            P("sec", None, None),
            P("ops", "sec", None, None),
            P("ops", "sec", None, None),
            P("ops", "sec"),
        ),
        out_specs=(P("sec", "ops", None), P("sec", "ops", None), P()),
        check_vma=False,
    )
```

```python
import functools

import jax
import jax.numpy as jnp
from jax import lax
from jax.experimental import pallas as pl
from jax.experimental.pallas import tpu as pltpu
from jax.sharding import PartitionSpec as P

STREAM_P = 40

VMEM_BYTES = 32 * 2**20

NT = (((1,), (1,)), ((), ()))
NN = (((1,), (0,)), ((), ()))


def log2(n):
    bits = n.bit_length() - 1
    assert n == 1 << bits
    return bits


def halving_orders(ops_bits, sec_bits):
    plane = [("ops", bit) for bit in range(1, ops_bits)]
    turned = plane[(ops_bits - 1) // 2 :] + plane[: (ops_bits - 1) // 2]
    sector = [("sec", bit) for bit in range(sec_bits)]
    return (
        (plane + sector, turned + sector),
        (sector[::-1] + plane, sector + turned),
    )


def places(order, axis):
    last = len(order) - 1
    return {bit: 1 << (last - step) for step, (name, bit) in enumerate(order) if name == axis}


def slot_part(order, axis, mask):
    return sum(((mask >> bit) & 1) * weight for bit, weight in places(order, axis).items())


def split(x):
    high = x.astype(jnp.bfloat16)
    low = (x - high.astype(jnp.float32)).astype(jnp.bfloat16)
    return high, low


def dot3(a, b_high, b_low, dims):
    a_high, a_low = split(a)
    rows = a.shape[0]
    both = lax.dot_general(
        jnp.concatenate([a_high, a_low], 0), b_high, dims, preferred_element_type=jnp.float32
    )
    cross = lax.dot_general(a_high, b_low, dims, preferred_element_type=jnp.float32)
    return both[:rows] + (both[rows:] + cross)


def sigma_kernel(orders, sectors, pieces, links_ref, psi_ref, lefts_ref, rights_ref, *rest):
    outs, (psi, lefts, rights, psi_high, psi_low, targets, sems) = rest[:4], rest[4:]
    pairs, _, rows, states = lefts.shape
    blocks = lefts.shape[1] // 2
    me = lax.axis_index("ops")
    core = me & 1
    psi_copy = pltpu.make_async_copy(psi_ref.at[0], psi, sems.at[2 * pairs])
    links_copy = pltpu.make_async_copy(links_ref, targets, sems.at[2 * pairs + 1])
    left_copies = [pltpu.make_async_copy(lefts_ref.at[p], lefts.at[p], sems.at[p]) for p in range(pairs)]
    right_copies = [pltpu.make_async_copy(rights_ref.at[p], rights.at[p], sems.at[pairs + p]) for p in range(pairs)]
    links_copy.start()
    psi_copy.start()
    for p in range(pairs):
        left_copies[p].start()
        right_copies[p].start()
    for out in outs:
        out[...] = jnp.zeros_like(out)
    links_copy.wait()
    psi_copy.wait()
    high, low = split(psi[...])
    psi_high[...] = high
    psi_low[...] = low

    def contribute(pair, away_sector):
        mine = jnp.concatenate(
            [lefts[pair, me ^ away ^ (block << 1)] for away in range(2) for block in range(blocks)], 0
        )
        product_left = dot3(mine, psi_high[...], psi_low[...], NN)
        right_high, right_low = split(rights[pair])
        product = dot3(product_left, right_high, right_low, NT)
        product = product.reshape(2, blocks, rows, states)
        start = 0
        for stream, piece in enumerate(pieces):
            for away in range(2):
                first = (core ^ away) == 0
                sector_part = jnp.where(
                    first,
                    slot_part(orders[stream][0], "sec", away_sector),
                    slot_part(orders[stream][1], "sec", away_sector),
                )
                for block in range(blocks):
                    block_part = jnp.where(
                        first,
                        slot_part(orders[stream][0], "ops", block << 1),
                        slot_part(orders[stream][1], "ops", block << 1),
                    )
                    outs[2 * stream + away][block_part + sector_part] += product[away, block, start : start + piece]
            start += piece

    for p in range(pairs):
        left_copies[p].wait()
        right_copies[p].wait()
        target = targets[p]

        @pl.when(target < sectors)
        def _():
            contribute(p, target ^ lax.axis_index("sec"))


def partial_sigma(psi, lefts, rights, links, pieces, orders, sectors):
    pairs, owners, rows, states = lefts.shape
    outs = [
        jax.ShapeDtypeStruct((owners // 2 * sectors, piece, states), jnp.float32) for piece in pieces for _ in range(2)
    ]
    return pl.pallas_call(
        functools.partial(sigma_kernel, orders, sectors, pieces),
        in_specs=[pl.BlockSpec(memory_space=pltpu.HBM)] * 4,
        out_specs=[pl.BlockSpec(memory_space=pltpu.VMEM)] * len(outs),
        out_shape=outs,
        scratch_shapes=[
            pltpu.VMEM((states, states), jnp.float32),
            pltpu.VMEM((pairs, owners, rows, states), jnp.float32),
            pltpu.VMEM((pairs, states, states), jnp.float32),
            pltpu.VMEM((states, states), jnp.bfloat16),
            pltpu.VMEM((states, states), jnp.bfloat16),
            pltpu.SMEM((pairs,), jnp.int32),
            pltpu.SemaphoreType.DMA((2 * pairs + 2,)),
        ],
        compiler_params=pltpu.CompilerParams(vmem_limit_bytes=VMEM_BYTES),
        cost_estimate=pl.CostEstimate(
            flops=12 * pairs * owners * rows * states * states,
            bytes_accessed=4 * states * states * (2 * pairs + 1),
            transcendentals=0,
        ),
        name="partial_sigma",
    )(*[pltpu.with_memory_space_constraint(x, pltpu.HBM) for x in (links, psi, lefts, rights)])


def stats_kernel(groups, psi_ref, *rest):
    ins, (sigma_ref, held_ref, psi_rows_ref, stats_ref, sem) = rest[:-5], rest[-5:]
    rows = sigma_ref.shape[1]
    copy = pltpu.make_async_copy(
        psi_ref.at[0, pl.ds(pl.multiple_of(lax.axis_index("ops") * rows, rows), rows)], psi_rows_ref, sem
    )
    copy.start()
    at = 0
    start = 0
    for group in groups:
        total = ins[at][...]
        for ref in ins[at + 1 : at + group]:
            total = total + ref[...]
        at += group
        total = total.reshape(total.shape[-2:])
        held_ref[start : start + total.shape[0]] = total
        start += total.shape[0]
    copy.wait()
    psi = psi_rows_ref[...]
    sigma = held_ref[...]
    sigma_ref[0] = sigma
    weight = jnp.sum(psi * psi)
    correlation = jnp.sum(psi * sigma)
    theta = jnp.where(weight > 0.0, correlation / weight, 0.0)
    residual = sigma - theta * psi
    squared = jnp.sum(residual * residual)
    lane = lax.broadcasted_iota(jnp.int32, stats_ref.shape, 1)
    stats_ref[...] = jnp.where(lane == 0, weight, jnp.where(lane == 1, theta, jnp.where(lane == 2, squared, 0.0)))


def finish_kernel(psi_ref, sigma_ref, stats_ref, direction_ref, energies_ref):
    weights = stats_ref[:, 0:1]
    thetas = stats_ref[:, 1:2]
    squares = stats_ref[:, 2:3]
    theta = jnp.sum(weights * thetas) / jnp.sum(weights)
    apart = thetas - theta
    norm = jnp.sqrt(jnp.sum(squares + weights * apart * apart))
    energies_ref[0] = theta
    energies_ref[1] = norm
    direction_ref[0] = (sigma_ref[...] - theta * psi_ref[...]) / norm


def halve(parts, orders, ops_width, sectors):
    for step in range(len(orders[0])):
        partner = []
        for ops in range(ops_width):
            axis, bit = orders[ops & 1][step]
            for sec in range(sectors):
                to = (ops ^ (1 << bit), sec) if axis == "ops" else (ops, sec ^ (1 << bit))
                partner.append((ops * sectors + sec, to[0] * sectors + to[1]))
        half = parts[0].shape[0] // 2
        leaving = sum(p[half:] for p in parts)
        parts = [p[:half] for p in parts] + [lax.ppermute(leaving, ("ops", "sec"), partner)]
    return [p[0] for p in parts]


def local(psi, left_ops, right_ops, links):
    ops_width = lax.axis_size("ops")
    sectors = lax.axis_size("sec")
    pairs, _, states, _ = left_ops.shape
    rows = states // ops_width
    lefts = left_ops.reshape(pairs, ops_width, rows, states)
    rights = right_ops.reshape(pairs, states, states)
    links = links.reshape(pairs)
    orders = halving_orders(log2(ops_width), log2(sectors))
    pieces = (STREAM_P, rows - STREAM_P) if rows > STREAM_P else (rows // 2, rows - rows // 2)
    keep_p, send_p, keep_q, send_q = partial_sigma(psi, lefts, rights, links, pieces, orders, sectors)
    swap = [(i, i ^ 1) for i in range(ops_width)]
    came_p = lax.ppermute(send_p, "ops", swap)
    came_q = lax.ppermute(send_q, "ops", swap)
    stream_p = halve([keep_p, came_p], orders[0], ops_width, sectors)
    stream_q = halve([keep_q, came_q], orders[1], ops_width, sectors)
    terms = stream_p + stream_q
    groups = [len(stream_p), len(stream_q)]
    devices = ops_width * sectors
    vmem = pl.BlockSpec(memory_space=pltpu.VMEM)
    sigma, held, psi_rows, stats = pl.pallas_call(
        functools.partial(stats_kernel, groups),
        in_specs=[pl.BlockSpec(memory_space=pltpu.HBM)] + [vmem] * len(terms),
        out_specs=[vmem] * 4,
        out_shape=[
            jax.ShapeDtypeStruct((1, rows, states), jnp.float32),
            jax.ShapeDtypeStruct((rows, states), jnp.float32),
            jax.ShapeDtypeStruct((rows, states), jnp.float32),
            jax.ShapeDtypeStruct((devices, 128), jnp.float32),
        ],
        scratch_shapes=[pltpu.SemaphoreType.DMA],
        compiler_params=pltpu.CompilerParams(vmem_limit_bytes=8 * 2**20),
        name="stats",
    )(psi, *terms)
    stats = lax.all_to_all(stats, ("ops", "sec"), 0, 0, tiled=True)
    direction, energies = pl.pallas_call(
        finish_kernel,
        in_specs=[vmem] * 3,
        out_specs=[vmem, pl.BlockSpec(memory_space=pltpu.SMEM)],
        out_shape=[
            jax.ShapeDtypeStruct((1, rows, states), jnp.float32),
            jax.ShapeDtypeStruct((2,), jnp.float32),
        ],
        compiler_params=pltpu.CompilerParams(vmem_limit_bytes=4 * 2**20),
        name="finish",
    )(psi_rows, held, stats)
    return (sigma, direction, energies)


def solution(mesh):
    return jax.shard_map(
        local,
        mesh=mesh,
        in_specs=(
            P("sec", None, None),
            P("ops", "sec", None, None),
            P("ops", "sec", None, None),
            P("ops", "sec"),
        ),
        out_specs=(P("sec", "ops", None), P("sec", "ops", None), P()),
        check_vma=False,
    )
```

```python
import functools

import jax
import jax.numpy as jnp
from jax import lax
from jax.experimental import pallas as pl
from jax.experimental.pallas import tpu as pltpu
from jax.sharding import PartitionSpec as P

STREAM_P = 40

VMEM_BYTES = 32 * 2**20

NT = (((1,), (1,)), ((), ()))
NN = (((1,), (0,)), ((), ()))


def log2(n):
    bits = n.bit_length() - 1
    assert n == 1 << bits
    return bits


def halving_orders(ops_bits, sec_bits):
    plane = [("ops", bit) for bit in range(1, ops_bits)]
    turned = plane[(ops_bits - 1) // 2 :] + plane[: (ops_bits - 1) // 2]
    sector = [("sec", bit) for bit in range(sec_bits)]
    return (
        (plane + sector, turned + sector),
        (sector[::-1] + plane, sector + plane),
    )


def places(order, axis):
    last = len(order) - 1
    return {bit: 1 << (last - step) for step, (name, bit) in enumerate(order) if name == axis}


def slot_part(order, axis, mask):
    return sum(((mask >> bit) & 1) * weight for bit, weight in places(order, axis).items())


def split(x):
    high = x.astype(jnp.bfloat16)
    low = (x - high.astype(jnp.float32)).astype(jnp.bfloat16)
    return high, low


def dot3(a, b_high, b_low, dims):
    a_high, a_low = split(a)
    rows = a.shape[0]
    both = lax.dot_general(
        jnp.concatenate([a_high, a_low], 0), b_high, dims, preferred_element_type=jnp.float32
    )
    cross = lax.dot_general(a_high, b_low, dims, preferred_element_type=jnp.float32)
    return both[:rows] + (both[rows:] + cross)


def sigma_kernel(orders, sectors, pieces, links_ref, psi_ref, lefts_ref, rights_ref, *rest):
    outs, (psi, lefts, rights, psi_high, psi_low, targets, sems) = rest[:6], rest[6:]
    stream_refs = ((outs[0:2], outs[2:4]), (outs[4:5], outs[5:6]))
    pairs, _, rows, states = lefts.shape
    blocks = lefts.shape[1] // 2
    me = lax.axis_index("ops")
    core = me & 1
    psi_copy = pltpu.make_async_copy(psi_ref.at[0], psi, sems.at[2 * pairs])
    links_copy = pltpu.make_async_copy(links_ref, targets, sems.at[2 * pairs + 1])
    left_copies = [pltpu.make_async_copy(lefts_ref.at[p], lefts.at[p], sems.at[p]) for p in range(pairs)]
    right_copies = [pltpu.make_async_copy(rights_ref.at[p], rights.at[p], sems.at[pairs + p]) for p in range(pairs)]
    links_copy.start()
    psi_copy.start()
    for p in range(pairs):
        left_copies[p].start()
        right_copies[p].start()
    for out in outs:
        out[...] = jnp.zeros_like(out)
    links_copy.wait()
    psi_copy.wait()
    high, low = split(psi[...])
    psi_high[...] = high
    psi_low[...] = low

    def contribute(pair, away_sector):
        mine = jnp.concatenate(
            [lefts[pair, me ^ away ^ (block << 1)] for away in range(2) for block in range(blocks)], 0
        )
        product_left = dot3(mine, psi_high[...], psi_low[...], NN)
        right_high, right_low = split(rights[pair])
        product = dot3(product_left, right_high, right_low, NT)
        product = product.reshape(2, blocks, rows, states)
        start = 0
        for stream, piece in enumerate(pieces):
            for away in range(2):
                first = (core ^ away) == 0
                sector_part = jnp.where(
                    first,
                    slot_part(orders[stream][0], "sec", away_sector),
                    slot_part(orders[stream][1], "sec", away_sector),
                )
                for block in range(blocks):
                    block_part = jnp.where(
                        first,
                        slot_part(orders[stream][0], "ops", block << 1),
                        slot_part(orders[stream][1], "ops", block << 1),
                    )
                    slot = block_part + sector_part
                    term = product[away, block, start : start + piece]
                    refs = stream_refs[stream][away]
                    if len(refs) == 1:
                        refs[0][slot] += term
                        continue
                    half = refs[0].shape[0]

                    @pl.when(slot < half)
                    def _():
                        refs[0][slot] += term

                    @pl.when(slot >= half)
                    def _():
                        refs[1][slot - half] += term

            start += piece

    for p in range(pairs):
        left_copies[p].wait()
        right_copies[p].wait()
        target = targets[p]

        @pl.when(target < sectors)
        def _():
            contribute(p, target ^ lax.axis_index("sec"))


def partial_sigma(psi, lefts, rights, links, pieces, orders, sectors):
    pairs, owners, rows, states = lefts.shape
    slots = owners // 2 * sectors
    outs = [jax.ShapeDtypeStruct((slots // 2, pieces[0], states), jnp.float32)] * 4
    outs += [jax.ShapeDtypeStruct((slots, pieces[1], states), jnp.float32)] * 2
    return pl.pallas_call(
        functools.partial(sigma_kernel, orders, sectors, pieces),
        in_specs=[pl.BlockSpec(memory_space=pltpu.HBM)] * 4,
        out_specs=[pl.BlockSpec(memory_space=pltpu.VMEM)] * len(outs),
        out_shape=outs,
        scratch_shapes=[
            pltpu.VMEM((states, states), jnp.float32),
            pltpu.VMEM((pairs, owners, rows, states), jnp.float32),
            pltpu.VMEM((pairs, states, states), jnp.float32),
            pltpu.VMEM((states, states), jnp.bfloat16),
            pltpu.VMEM((states, states), jnp.bfloat16),
            pltpu.SMEM((pairs,), jnp.int32),
            pltpu.SemaphoreType.DMA((2 * pairs + 2,)),
        ],
        compiler_params=pltpu.CompilerParams(vmem_limit_bytes=VMEM_BYTES),
        cost_estimate=pl.CostEstimate(
            flops=12 * pairs * owners * rows * states * states,
            bytes_accessed=4 * states * states * (2 * pairs + 1),
            transcendentals=0,
        ),
        name="partial_sigma",
    )(*[pltpu.with_memory_space_constraint(x, pltpu.HBM) for x in (links, psi, lefts, rights)])


def stats_kernel(groups, psi_ref, *rest):
    ins, (sigma_ref, held_ref, psi_rows_ref, stats_ref, sem) = rest[:-5], rest[-5:]
    rows = sigma_ref.shape[1]
    copy = pltpu.make_async_copy(
        psi_ref.at[0, pl.ds(pl.multiple_of(lax.axis_index("ops") * rows, rows), rows)], psi_rows_ref, sem
    )
    copy.start()
    at = 0
    start = 0
    for group in groups:
        total = ins[at][...]
        for ref in ins[at + 1 : at + group]:
            total = total + ref[...]
        at += group
        total = total.reshape(total.shape[-2:])
        held_ref[start : start + total.shape[0]] = total
        start += total.shape[0]
    copy.wait()
    psi = psi_rows_ref[...]
    sigma = held_ref[...]
    sigma_ref[0] = sigma
    weight = jnp.sum(psi * psi)
    correlation = jnp.sum(psi * sigma)
    theta = jnp.where(weight > 0.0, correlation / weight, 0.0)
    residual = sigma - theta * psi
    squared = jnp.sum(residual * residual)
    lane = lax.broadcasted_iota(jnp.int32, stats_ref.shape, 1)
    stats_ref[...] = jnp.where(lane == 0, weight, jnp.where(lane == 1, theta, jnp.where(lane == 2, squared, 0.0)))


def finish_kernel(psi_ref, sigma_ref, stats_ref, direction_ref, energies_ref):
    weights = stats_ref[:, 0:1]
    thetas = stats_ref[:, 1:2]
    squares = stats_ref[:, 2:3]
    theta = jnp.sum(weights * thetas) / jnp.sum(weights)
    apart = thetas - theta
    norm = jnp.sqrt(jnp.sum(squares + weights * apart * apart))
    energies_ref[0] = theta
    energies_ref[1] = norm
    direction_ref[0] = (sigma_ref[...] - theta * psi_ref[...]) / norm


def after(value, earlier):
    return lax.optimization_barrier((value, earlier))[0]


def halving_step(leaving, orders, step, ops_width, sectors):
    partner = []
    for ops in range(ops_width):
        axis, bit = orders[ops & 1][step]
        for sec in range(sectors):
            to = (ops ^ (1 << bit), sec) if axis == "ops" else (ops, sec ^ (1 << bit))
            partner.append((ops * sectors + sec, to[0] * sectors + to[1]))
    return lax.ppermute(leaving, ("ops", "sec"), partner)


def leaving_of(parts):
    half = parts[0].shape[0] // 2
    return sum(p[half:] for p in parts)


def staying_of(parts):
    half = parts[0].shape[0] // 2
    return [p[:half] for p in parts]


def local(psi, left_ops, right_ops, links):
    ops_width = lax.axis_size("ops")
    sectors = lax.axis_size("sec")
    pairs, _, states, _ = left_ops.shape
    rows = states // ops_width
    lefts = left_ops.reshape(pairs, ops_width, rows, states)
    rights = right_ops.reshape(pairs, states, states)
    links = links.reshape(pairs)
    orders = halving_orders(log2(ops_width), log2(sectors))
    pieces = (STREAM_P, rows - STREAM_P) if rows > STREAM_P else (rows // 2, rows - rows // 2)
    keep_low, keep_high, send_low, send_high, keep_q, send_q = partial_sigma(
        psi, lefts, rights, links, pieces, orders, sectors
    )
    swap = [(i, i ^ 1) for i in range(ops_width)]
    came_high, came_low, came_q = [lax.ppermute(x, "ops", swap) for x in (send_high, send_low, send_q)]
    parts_q = [keep_q, came_q]
    leaving_p, stream_p = keep_high + came_high, [keep_low, came_low]
    leaving_q, stream_q = leaving_of(parts_q), staying_of(parts_q)
    for step in range(len(orders[0][0])):
        if step:
            before = leaving_q
            leaving_p, stream_p = leaving_of(stream_p), staying_of(stream_p)
            leaving_q, stream_q = leaving_of(stream_q), staying_of(stream_q)
            leaving_q = after(leaving_q, leaving_p)
            if step > 1:
                leaving_p = after(leaving_p, before)
        stream_p = stream_p + [halving_step(leaving_p, orders[0], step, ops_width, sectors)]
        stream_q = stream_q + [halving_step(leaving_q, orders[1], step, ops_width, sectors)]
    terms = [p[0] for p in stream_p + stream_q]
    groups = [len(stream_p), len(stream_q)]
    devices = ops_width * sectors
    vmem = pl.BlockSpec(memory_space=pltpu.VMEM)
    sigma, held, psi_rows, stats = pl.pallas_call(
        functools.partial(stats_kernel, groups),
        in_specs=[pl.BlockSpec(memory_space=pltpu.HBM)] + [vmem] * len(terms),
        out_specs=[vmem] * 4,
        out_shape=[
            jax.ShapeDtypeStruct((1, rows, states), jnp.float32),
            jax.ShapeDtypeStruct((rows, states), jnp.float32),
            jax.ShapeDtypeStruct((rows, states), jnp.float32),
            jax.ShapeDtypeStruct((devices, 128), jnp.float32),
        ],
        scratch_shapes=[pltpu.SemaphoreType.DMA],
        compiler_params=pltpu.CompilerParams(vmem_limit_bytes=8 * 2**20),
        name="stats",
    )(psi, *terms)
    stats = lax.all_to_all(stats, ("ops", "sec"), 0, 0, tiled=True)
    direction, energies = pl.pallas_call(
        finish_kernel,
        in_specs=[vmem] * 3,
        out_specs=[vmem, pl.BlockSpec(memory_space=pltpu.SMEM)],
        out_shape=[
            jax.ShapeDtypeStruct((1, rows, states), jnp.float32),
            jax.ShapeDtypeStruct((2,), jnp.float32),
        ],
        compiler_params=pltpu.CompilerParams(vmem_limit_bytes=4 * 2**20),
        name="finish",
    )(psi_rows, held, stats)
    return (sigma, direction, energies)


def solution(mesh):
    return jax.shard_map(
        local,
        mesh=mesh,
        in_specs=(
            P("sec", None, None),
            P("ops", "sec", None, None),
            P("ops", "sec", None, None),
            P("ops", "sec"),
        ),
        out_specs=(P("sec", "ops", None), P("sec", "ops", None), P()),
        check_vma=False,
    )
```

```python
import functools

import jax
import jax.numpy as jnp
from jax import lax
from jax.experimental import pallas as pl
from jax.experimental.pallas import tpu as pltpu
from jax.sharding import PartitionSpec as P

STREAM_P = 40

VMEM_BYTES = 32 * 2**20

NT = (((1,), (1,)), ((), ()))
NN = (((1,), (0,)), ((), ()))


def log2(n):
    bits = n.bit_length() - 1
    assert n == 1 << bits
    return bits


def halving_orders(ops_bits, sec_bits):
    plane = [("ops", bit) for bit in range(1, ops_bits)]
    turned = plane[(ops_bits - 1) // 2 :] + plane[: (ops_bits - 1) // 2]
    sector = [("sec", bit) for bit in range(sec_bits)]
    return (
        (plane + sector, turned + sector),
        (sector[::-1] + plane, sector + plane),
    )


def places(order, axis):
    last = len(order) - 1
    return {bit: 1 << (last - step) for step, (name, bit) in enumerate(order) if name == axis}


def slot_part(order, axis, mask):
    return sum(((mask >> bit) & 1) * weight for bit, weight in places(order, axis).items())


def split(x):
    high = x.astype(jnp.bfloat16)
    low = (x - high.astype(jnp.float32)).astype(jnp.bfloat16)
    return high, low


def dot3(a, b_high, b_low, dims):
    a_high, a_low = split(a)
    rows = a.shape[0]
    both = lax.dot_general(
        jnp.concatenate([a_high, a_low], 0), b_high, dims, preferred_element_type=jnp.float32
    )
    cross = lax.dot_general(a_high, b_low, dims, preferred_element_type=jnp.float32)
    return both[:rows] + (both[rows:] + cross)


def sigma_kernel(orders, sectors, pieces, links_ref, psi_ref, lefts_ref, rights_ref, *rest):
    outs, (psi, lefts, rights, psi_high, psi_low, targets, sems) = rest[:6], rest[6:]
    stream_refs = ((outs[0:2], outs[2:4]), (outs[4:5], outs[5:6]))
    pairs, _, rows, states = lefts.shape
    blocks = lefts.shape[1] // 2
    me = lax.axis_index("ops")
    core = me & 1
    psi_copy = pltpu.make_async_copy(psi_ref.at[0], psi, sems.at[2 * pairs])
    links_copy = pltpu.make_async_copy(links_ref, targets, sems.at[2 * pairs + 1])
    left_copies = [pltpu.make_async_copy(lefts_ref.at[p], lefts.at[p], sems.at[p]) for p in range(pairs)]
    right_copies = [pltpu.make_async_copy(rights_ref.at[p], rights.at[p], sems.at[pairs + p]) for p in range(pairs)]
    links_copy.start()
    psi_copy.start()
    for p in range(pairs):
        left_copies[p].start()
        right_copies[p].start()
    for out in outs:
        out[...] = jnp.zeros_like(out)
    links_copy.wait()
    psi_copy.wait()
    high, low = split(psi[...])
    psi_high[...] = high
    psi_low[...] = low

    def contribute(pair, away_sector):
        mine = jnp.concatenate(
            [lefts[pair, me ^ away ^ (block << 1)] for away in range(2) for block in range(blocks)], 0
        )
        product_left = dot3(mine, psi_high[...], psi_low[...], NN)
        right_high, right_low = split(rights[pair])
        product = dot3(product_left, right_high, right_low, NT)
        product = product.reshape(2, blocks, rows, states)
        start = 0
        for stream, piece in enumerate(pieces):
            for away in range(2):
                first = (core ^ away) == 0
                sector_part = jnp.where(
                    first,
                    slot_part(orders[stream][0], "sec", away_sector),
                    slot_part(orders[stream][1], "sec", away_sector),
                )
                for block in range(blocks):
                    block_part = jnp.where(
                        first,
                        slot_part(orders[stream][0], "ops", block << 1),
                        slot_part(orders[stream][1], "ops", block << 1),
                    )
                    slot = block_part + sector_part
                    term = product[away, block, start : start + piece]
                    refs = stream_refs[stream][away]
                    if len(refs) == 1:
                        refs[0][slot] += term
                        continue
                    half = refs[0].shape[0]

                    @pl.when(slot < half)
                    def _():
                        refs[0][slot] += term

                    @pl.when(slot >= half)
                    def _():
                        refs[1][slot - half] += term

            start += piece

    for p in range(pairs):
        left_copies[p].wait()
        right_copies[p].wait()
        target = targets[p]

        @pl.when(target < sectors)
        def _():
            contribute(p, target ^ lax.axis_index("sec"))


def partial_sigma(psi, lefts, rights, links, pieces, orders, sectors):
    pairs, owners, rows, states = lefts.shape
    slots = owners // 2 * sectors
    outs = [jax.ShapeDtypeStruct((slots // 2, pieces[0], states), jnp.float32)] * 4
    outs += [jax.ShapeDtypeStruct((slots, pieces[1], states), jnp.float32)] * 2
    return pl.pallas_call(
        functools.partial(sigma_kernel, orders, sectors, pieces),
        in_specs=[pl.BlockSpec(memory_space=pltpu.HBM)] * 4,
        out_specs=[pl.BlockSpec(memory_space=pltpu.VMEM)] * len(outs),
        out_shape=outs,
        scratch_shapes=[
            pltpu.VMEM((states, states), jnp.float32),
            pltpu.VMEM((pairs, owners, rows, states), jnp.float32),
            pltpu.VMEM((pairs, states, states), jnp.float32),
            pltpu.VMEM((states, states), jnp.bfloat16),
            pltpu.VMEM((states, states), jnp.bfloat16),
            pltpu.SMEM((pairs,), jnp.int32),
            pltpu.SemaphoreType.DMA((2 * pairs + 2,)),
        ],
        compiler_params=pltpu.CompilerParams(vmem_limit_bytes=VMEM_BYTES),
        cost_estimate=pl.CostEstimate(
            flops=12 * pairs * owners * rows * states * states,
            bytes_accessed=4 * states * states * (2 * pairs + 1),
            transcendentals=0,
        ),
        name="partial_sigma",
    )(*[pltpu.with_memory_space_constraint(x, pltpu.HBM) for x in (links, psi, lefts, rights)])


def stats_kernel(groups, psi_ref, *rest):
    ins, (held_ref, psi_rows_ref, stats_ref, sem) = rest[:-4], rest[-4:]
    rows = held_ref.shape[0]
    copy = pltpu.make_async_copy(
        psi_ref.at[0, pl.ds(pl.multiple_of(lax.axis_index("ops") * rows, rows), rows)], psi_rows_ref, sem
    )
    copy.start()
    at = 0
    start = 0
    for group in groups:
        total = ins[at][...]
        for ref in ins[at + 1 : at + group]:
            total = total + ref[...]
        at += group
        total = total.reshape(total.shape[-2:])
        held_ref[start : start + total.shape[0]] = total
        start += total.shape[0]
    copy.wait()
    psi = psi_rows_ref[...]
    sigma = held_ref[...]
    weight = jnp.sum(psi * psi)
    correlation = jnp.sum(psi * sigma)
    theta = jnp.where(weight > 0.0, correlation / weight, 0.0)
    residual = sigma - theta * psi
    squared = jnp.sum(residual * residual)
    lane = lax.broadcasted_iota(jnp.int32, stats_ref.shape, 1)
    stats_ref[...] = jnp.where(lane == 0, weight, jnp.where(lane == 1, theta, jnp.where(lane == 2, squared, 0.0)))


def finish_kernel(psi_ref, held_ref, stats_ref, sigma_ref, direction_ref, energies_ref):
    sigma_ref[0] = held_ref[...]
    weights = stats_ref[:, 0:1]
    thetas = stats_ref[:, 1:2]
    squares = stats_ref[:, 2:3]
    theta = jnp.sum(weights * thetas) / jnp.sum(weights)
    apart = thetas - theta
    norm = jnp.sqrt(jnp.sum(squares + weights * apart * apart))
    energies_ref[0] = theta
    energies_ref[1] = norm
    direction_ref[0] = (held_ref[...] - theta * psi_ref[...]) / norm


def after(value, earlier):
    return lax.optimization_barrier((value, earlier))[0]


def halving_step(leaving, orders, step, ops_width, sectors):
    partner = []
    for ops in range(ops_width):
        axis, bit = orders[ops & 1][step]
        for sec in range(sectors):
            to = (ops ^ (1 << bit), sec) if axis == "ops" else (ops, sec ^ (1 << bit))
            partner.append((ops * sectors + sec, to[0] * sectors + to[1]))
    return lax.ppermute(leaving, ("ops", "sec"), partner)


def leaving_of(parts):
    half = parts[0].shape[0] // 2
    return sum(p[half:] for p in parts)


def staying_of(parts):
    half = parts[0].shape[0] // 2
    return [p[:half] for p in parts]


def local(psi, left_ops, right_ops, links):
    ops_width = lax.axis_size("ops")
    sectors = lax.axis_size("sec")
    pairs, _, states, _ = left_ops.shape
    rows = states // ops_width
    lefts = left_ops.reshape(pairs, ops_width, rows, states)
    rights = right_ops.reshape(pairs, states, states)
    links = links.reshape(pairs)
    orders = halving_orders(log2(ops_width), log2(sectors))
    pieces = (STREAM_P, rows - STREAM_P) if rows > STREAM_P else (rows // 2, rows - rows // 2)
    keep_low, keep_high, send_low, send_high, keep_q, send_q = partial_sigma(
        psi, lefts, rights, links, pieces, orders, sectors
    )
    swap = [(i, i ^ 1) for i in range(ops_width)]
    came_high, came_low, came_q = [lax.ppermute(x, "ops", swap) for x in (send_high, send_low, send_q)]
    parts_q = [keep_q, came_q]
    leaving_p, stream_p = keep_high + came_high, [keep_low, came_low]
    leaving_q, stream_q = leaving_of(parts_q), staying_of(parts_q)
    for step in range(len(orders[0][0])):
        if step:
            before = leaving_q
            leaving_p, stream_p = leaving_of(stream_p), staying_of(stream_p)
            leaving_q, stream_q = leaving_of(stream_q), staying_of(stream_q)
            leaving_q = after(leaving_q, leaving_p)
            if step > 1:
                leaving_p = after(leaving_p, before)
        stream_p = stream_p + [halving_step(leaving_p, orders[0], step, ops_width, sectors)]
        stream_q = stream_q + [halving_step(leaving_q, orders[1], step, ops_width, sectors)]
    terms = [p[0] for p in stream_p + stream_q]
    groups = [len(stream_p), len(stream_q)]
    devices = ops_width * sectors
    vmem = pl.BlockSpec(memory_space=pltpu.VMEM)
    held, psi_rows, stats = pl.pallas_call(
        functools.partial(stats_kernel, groups),
        in_specs=[pl.BlockSpec(memory_space=pltpu.HBM)] + [vmem] * len(terms),
        out_specs=[vmem] * 3,
        out_shape=[
            jax.ShapeDtypeStruct((rows, states), jnp.float32),
            jax.ShapeDtypeStruct((rows, states), jnp.float32),
            jax.ShapeDtypeStruct((devices, 128), jnp.float32),
        ],
        scratch_shapes=[pltpu.SemaphoreType.DMA],
        compiler_params=pltpu.CompilerParams(vmem_limit_bytes=8 * 2**20),
        name="stats",
    )(psi, *terms)
    stats = lax.all_to_all(stats, ("ops", "sec"), 0, 0, tiled=True)
    sigma, direction, energies = pl.pallas_call(
        finish_kernel,
        in_specs=[vmem] * 3,
        out_specs=[vmem, vmem, pl.BlockSpec(memory_space=pltpu.SMEM)],
        out_shape=[
            jax.ShapeDtypeStruct((1, rows, states), jnp.float32),
            jax.ShapeDtypeStruct((1, rows, states), jnp.float32),
            jax.ShapeDtypeStruct((2,), jnp.float32),
        ],
        compiler_params=pltpu.CompilerParams(vmem_limit_bytes=4 * 2**20),
        name="finish",
    )(psi_rows, held, stats)
    return (sigma, direction, energies)


def solution(mesh):
    return jax.shard_map(
        local,
        mesh=mesh,
        in_specs=(
            P("sec", None, None),
            P("ops", "sec", None, None),
            P("ops", "sec", None, None),
            P("ops", "sec"),
        ),
        out_specs=(P("sec", "ops", None), P("sec", "ops", None), P()),
        check_vma=False,
    )
```
